32 devices in a mesh: row: 4 (over z), col: 8 (over y, x, core).
Axes of the slice: x: 2, y: 2, z: 4, core: 2. Of those that a mesh axis runs over, the one named last changes fastest.
Arguments:
- inverse: float32 [16384, 16384], P('row', 'col'), may hold values from -0.0625 to 0.0625
- pattern: int32 [128, 128], P('row', 'col'), may hold values 0 or 1
- factor_first: float32 [16384, 256], P('col'), may hold values from -1.5 to 1.5
- factor_second: float32 [16384, 256], P('col'), may hold values from -1.5 to 1.5
- rows_first: int32 [64], replicated, may hold values from 0 to 127, as said below
- rows_second: int32 [64], replicated, may hold values from 0 to 127, as said below
- coupling: float32 [256, 256], replicated, may hold values from -0.375 to 0.375
- diag_first: float32 [256, 256], replicated, may hold values from -6 to 6
- diag_second: float32 [256, 256], replicated, may hold values from -6 to 6
Outputs:
- panel_one: float32 [16384, 256], P(('row', 'col'))
- panel_two: float32 [16384, 256], P(('row', 'col'))
- block_one: float32 [256, 256], replicated
- block_cross: float32 [256, 256], replicated
- block_two: float32 [256, 256], replicated
The draws below stay inside these ranges and needn't reach their ends.
Inputs may be any that keep to these rules, and one draw needn't show every extreme that they name: `rows_first`: 64 distinct block indices in increasing order; the first block, the block 64 and the last block are always among them. `rows_second`: 64 distinct block indices in increasing order; the first block, the block 64 and the last block are always among them.
All inputs are finite; a program needn't handle non-finite values. No bound on the sum of `pattern` on one device may be relied on, other than what follows from the above.
Results may differ from the reference program's by a relative error of at most 0.000071.
Values sent between devices are 32-bit elements; how exact they have to be, the bound alone decides.
No kernel may reach another device: no remote copies, remote signals or barrier semaphores. Data moves between devices by JAX's collectives and lax.ppermute only.
A program may use at most 192 MiB of HBM per device.

```python
import jax
import jax.numpy as jnp
from jax import lax

M = 16384
W = 256
BLK = 128
MB = 128
NB = 64


def chosen_blocks(key, salt):
    middle = MB // 2
    inner = jax.random.permutation(jax.random.fold_in(key, salt), MB - 3)[:NB - 3].astype(jnp.int32) + 1
    inner = jnp.where(inner >= middle, inner + 1, inner)
    picked = jnp.concatenate([jnp.array([0, middle, MB - 1], jnp.int32), inner])
    return jnp.sort(picked)


def draw_rows_first(key, part):
    return chosen_blocks(key, 17)


def draw_rows_second(key, part):
    return chosen_blocks(key, 29)


def touch_ends(result, own_key, least, largest):
    index_at = [jax.random.randint(jax.random.fold_in(own_key, axis), (), 0, length) for axis, length in enumerate(result.shape)]
    longest = result.shape.index(max(result.shape))
    beside = index_at[:longest] + [(index_at[longest] + 1) % result.shape[longest]] + index_at[longest + 1:]
    return result.at[tuple(index_at)].set(least).at[tuple(beside)].set(largest)


def steps_of(key, extent, split, smallest, top_value):
    def one(axis_at, blocks):
        heights = jax.random.uniform(jax.random.fold_in(jax.random.fold_in(key, 6), axis_at), (blocks,), jnp.float32, smallest / len(split), top_value / len(split))
        return jnp.repeat(jnp.exp(heights), extent[axis_at] // blocks).reshape((-1,) + (1,) * (len(extent) - axis_at - 1))

    factor_of = one(*split[0])
    for cut in split[1:]:
        factor_of = factor_of * one(*cut)
    return factor_of


def noise(stream_key, shape, spread, limit, pieces=(), kind=jnp.bfloat16):
    result = spread * jax.random.normal(stream_key, shape, jnp.float32)
    if pieces:
        result = result * steps_of(stream_key, shape, pieces, -0.22, 0.18)
    return jnp.clip(result, -limit, limit).astype(kind)


def setup_inputs(seed: int = 0) -> dict:
    keys = jax.random.split(jax.random.key(seed), 10)
    return {
        "inverse": noise(keys[0], (M, M), (M // 2) ** -0.5, 0.0625, ((0, 4), (1, 8)), jnp.float32),
        "pattern": touch_ends((jax.random.randint(keys[1], (MB, MB), 0, 8) < 5).astype(jnp.int32), jax.random.fold_in(keys[1], 1), 0, 1),
        "factor_first": noise(keys[2], (M, W), 0.25, 1.5, ((0, 8),), jnp.float32),
        "factor_second": noise(keys[3], (M, W), 0.25, 1.5, ((0, 8),), jnp.float32),
        "rows_first": draw_rows_first(jax.random.fold_in(keys[9], 71), 0),
        "rows_second": draw_rows_second(jax.random.fold_in(keys[9], 71), 0),
        "coupling": noise(keys[6], (W, W), W ** -0.5, 0.375, (), jnp.float32),
        "diag_first": noise(keys[7], (W, W), 1.0, 6.0, (), jnp.float32),
        "diag_second": noise(keys[8], (W, W), 1.0, 6.0, (), jnp.float32),
    }


def row_keep(rows_list):
    block_ids = jnp.arange(MB, dtype=jnp.int32)
    hits = jnp.sum((block_ids[:, None] == rows_list[None, :]).astype(jnp.float32), axis=1)
    return jnp.repeat(hits, BLK)


def reference(inverse, pattern, factor_first, factor_second, rows_first, rows_second, coupling, diag_first, diag_second):
    high = lax.Precision.HIGHEST
    masked = (inverse.reshape(MB, BLK, MB, BLK) * pattern.astype(jnp.float32)[:, None, :, None]).reshape(M, M)
    x_one = factor_first * row_keep(rows_first)[:, None]
    x_two = factor_second * row_keep(rows_second)[:, None]
    panel_one = -jnp.dot(masked, x_one, precision=high)
    block_one = diag_first - jnp.dot(x_one.T, panel_one, precision=high)
    panel_two = -(jnp.dot(masked, x_two, precision=high) + jnp.dot(panel_one, coupling, precision=high))
    block_cross = -(jnp.dot(panel_one.T, x_two, precision=high) + jnp.dot(block_one, coupling, precision=high))
    block_two = diag_second - jnp.dot(x_two.T, panel_two, precision=high) - jnp.dot(coupling.T, block_cross, precision=high)
    return (panel_one, panel_two, block_one, block_cross, block_two)
```

```python
import functools

import jax
import jax.numpy as jnp
from jax import lax
from jax.experimental import pallas as pl
from jax.experimental.pallas import tpu as pltpu
from jax.sharding import PartitionSpec as P

BLK = 128
AXES = ("row", "col")
F32 = jnp.float32
BF16 = jnp.bfloat16
VMEM_LIMIT = 48 * 1024 * 1024


def halves(value):
    high = value.astype(BF16)
    low = (value - high.astype(F32)).astype(BF16)
    return high, low


def dot3(a, b, dims=(((1,), (0,)), ((), ()))):
    a_high, a_low = halves(a)
    b_high, b_low = halves(b)
    mul = functools.partial(lax.dot_general, dimension_numbers=dims, preferred_element_type=F32)
    return mul(a_high, b_high) + (mul(a_high, b_low) + mul(a_low, b_high))


ROWS_DIM = (((0,), (0,)), ((), ()))


def member(block_ids, rows_list):
    hits = (block_ids[:, None] == rows_list[None, :]).astype(F32)
    return jnp.sum(hits, axis=1)


def prepare_body(first_ref, second_ref, keep_ref, high_ref, low_ref):
    width = first_ref.shape[1]
    for at, ref in enumerate((first_ref, second_ref)):
        high, low = halves(ref[...] * keep_ref[:, at : at + 1])
        high_ref[:, at * width : (at + 1) * width] = high
        low_ref[:, at * width : (at + 1) * width] = low


def prepare(first, second, keep):
    rows, width = first.shape
    tile = min(rows, 512)
    spec = lambda cols: pl.BlockSpec((tile, cols), lambda i: (i, 0))
    return pl.pallas_call(
        prepare_body,
        grid=(rows // tile,),
        in_specs=[spec(width), spec(width), spec(2)],
        out_specs=[spec(2 * width)] * 2,
        out_shape=[jax.ShapeDtypeStruct((rows, 2 * width), BF16)] * 2,
        compiler_params=pltpu.CompilerParams(vmem_limit_bytes=VMEM_LIMIT),
        name="prepare",
    )(first, second, keep)


def product_body(at_ref, a_ref, mask_ref, high_ref, low_ref, *rest):
    out_ref = rest[-1]
    tile, depth = a_ref.shape
    block0 = at_ref[0] * (tile // BLK) + pl.program_id(0) * (tile // BLK)
    parts = []
    for block in range(tile // BLK):
        mask = mask_ref[pl.ds(block0 + block, 1), :]
        parts.append(a_ref[block * BLK : (block + 1) * BLK, :] * mask)
    a = jnp.concatenate(parts, axis=0) if len(parts) > 1 else parts[0]
    a_high, a_low = halves(a)
    mul = functools.partial(jnp.dot, preferred_element_type=F32)
    out = mul(a_high, high_ref[...]) + mul(a_high, low_ref[...]) + mul(a_low, high_ref[...])
    if len(rest) > 1:
        out = out + rest[0][...]
    out_ref[...] = out


def product(inverse, mask, high, low, piece, piece_rows, add=None, tile=256):
    depth, width = high.shape
    tile = min(tile, piece_rows)
    steps = piece_rows // tile
    whole = lambda shape: pl.BlockSpec(shape, lambda i, at: (0, 0), pipeline_mode=pl.Buffered(1))
    out_spec = pl.BlockSpec((tile, width), lambda i, at: (i, 0))
    extra = [] if add is None else [add]
    return pl.pallas_call(
        product_body,
        grid_spec=pltpu.PrefetchScalarGridSpec(
            num_scalar_prefetch=1,
            grid=(steps,),
            in_specs=[
                pl.BlockSpec((tile, depth), lambda i, at: (at[0] + i, 0)),
                whole(mask.shape),
                whole(high.shape),
                whole(low.shape),
            ]
            + [out_spec] * len(extra),
            out_specs=out_spec,
        ),
        out_shape=jax.ShapeDtypeStruct((piece_rows, width), F32),
        compiler_params=pltpu.CompilerParams(vmem_limit_bytes=VMEM_LIMIT),
        cost_estimate=pl.CostEstimate(
            flops=6 * piece_rows * depth * width,
            bytes_accessed=4 * piece_rows * (depth + width),
            transcendentals=0,
        ),
        name="product",
    )((piece * steps).astype(jnp.int32).reshape(1), inverse, mask, high, low, *extra)


def finish_body(near_ref, keep_ref, coupling_ref, own_ref, *rest):
    *added, one_ref, two_ref, sums_ref = rest
    total = own_ref[...]
    for ref in added:
        total = total + ref[...]
    width = coupling_ref.shape[0]
    x_one = near_ref[0] * keep_ref[:, 0:1]
    x_two = near_ref[1] * keep_ref[:, 1:2]
    one = -total[:, :width]
    two = -(total[:, width:] + dot3(one, coupling_ref[...]))
    one_ref[...] = one
    two_ref[...] = two
    sums_ref[:width] = dot3(x_one, one, ROWS_DIM)
    sums_ref[width : 2 * width] = dot3(one, x_two, ROWS_DIM)
    sums_ref[2 * width :] = dot3(x_two, two, ROWS_DIM)


def finish(near, keep, coupling, own, added):
    rows = own.shape[0]
    width = coupling.shape[0]
    return pl.pallas_call(
        finish_body,
        out_shape=[
            jax.ShapeDtypeStruct((rows, width), F32),
            jax.ShapeDtypeStruct((rows, width), F32),
            jax.ShapeDtypeStruct((3 * width, width), F32),
        ],
        compiler_params=pltpu.CompilerParams(vmem_limit_bytes=VMEM_LIMIT),
        name="finish",
    )(near, keep, coupling, own, *added)


def close_body(sums_ref, coupling_ref, first_ref, second_ref, one_ref, cross_ref, two_ref):
    width = coupling_ref.shape[0]
    coupling = coupling_ref[...]
    one = first_ref[...] - sums_ref[:width]
    cross = -(sums_ref[width : 2 * width] + dot3(one, coupling))
    one_ref[...] = one
    cross_ref[...] = cross
    two_ref[...] = second_ref[...] - sums_ref[2 * width :] - dot3(coupling, cross, ROWS_DIM)


def close(sums, coupling, diag_first, diag_second):
    return pl.pallas_call(
        close_body,
        out_shape=[jax.ShapeDtypeStruct(coupling.shape, F32)] * 3,
        compiler_params=pltpu.CompilerParams(vmem_limit_bytes=VMEM_LIMIT),
        name="close",
    )(sums, coupling, diag_first, diag_second)


def flip(value, count, mask_of):
    return lax.ppermute(value, AXES, [(i, i ^ mask_of(i)) for i in range(count)])


def bits_of(count):
    return count.bit_length() - 1


def total_over_all(value, rows, cols, me):
    count = rows * cols
    order = [1 << bit for bit in range(bits_of(count))]
    for bit in order:
        half = value.shape[0] // 2
        mine = ((me & bit) != 0).astype(jnp.int32)
        sent = lax.dynamic_slice_in_dim(value, (1 - mine) * half, half, 0)
        kept = lax.dynamic_slice_in_dim(value, mine * half, half, 0)
        value = kept + flip(sent, count, lambda i: bit)
    for bit in reversed(order):
        other = flip(value, count, lambda i: bit)
        low = (me & bit) == 0
        value = jnp.concatenate(
            [jnp.where(low, value, other), jnp.where(low, other, value)], axis=0
        )
    return value


def per_device(
    inverse,
    pattern,
    factor_first,
    factor_second,
    rows_first,
    rows_second,
    coupling,
    diag_first,
    diag_second,
):
    row_count = lax.axis_size("row")
    col_count = lax.axis_size("col")
    count = row_count * col_count
    row_index = lax.axis_index("row")
    col_index = lax.axis_index("col")
    me = row_index * col_count + col_index
    share_rows = factor_first.shape[0]
    local_rows, local_cols = inverse.shape
    quota_rows = local_rows // col_count

    piece_at = row_index ^ (col_index & (row_count - 1))
    outgoing = jnp.stack(
        [
            lax.dynamic_slice_in_dim(factor, piece_at * quota_rows, quota_rows, 0)
            for factor in (factor_first, factor_second)
        ]
    )
    moves = []
    for k in range(row_count):
        for c in range(col_count):
            moves.append((k * col_count + c, c * row_count + (k ^ (c & (row_count - 1)))))
    near = lax.ppermute(outgoing, AXES, moves)

    def keep_of(start, rows):
        ids = (start + jnp.arange(rows, dtype=jnp.int32)) // BLK
        return jnp.stack([member(ids, rows_first), member(ids, rows_second)], axis=1)

    keep = keep_of(col_index * share_rows, share_rows)
    near_keep = keep_of(me * quota_rows, quota_rows)
    mask = jnp.repeat(pattern.astype(F32), BLK, axis=1)
    high, low = prepare(factor_first, factor_second, keep)

    core = col_index & 1
    spare = bits_of(col_count) - 1
    forward = [2 << bit for bit in range(spare)]
    backward = list(reversed(forward))
    arrived = {e: [] for e in range(1 << spare)}
    order = sorted(arrived, key=lambda e: -int(format(e, "b").zfill(spare)[::-1] or "0", 2))
    own = None
    for e in order:
        offsets = [
            sum(bit for at, bit in enumerate(line) if e >> at & 1) for line in (forward, backward)
        ]
        mine = col_index ^ jnp.where(core == 0, offsets[0], offsets[1])
        theirs = col_index ^ 1 ^ jnp.where(core == 1, offsets[0], offsets[1])
        partner = product(inverse, mask, high, low, theirs, quota_rows)
        partner = flip(partner, count, lambda i: 1)
        total = product(inverse, mask, high, low, mine, quota_rows)
        total = total + partner
        for part in arrived[e]:
            total = total + part
        if e:
            at = (e & -e).bit_length() - 1
            got = flip(total, count, lambda i: (backward if i & 1 else forward)[at])
            arrived[e & (e - 1)].append(got)
        else:
            own = total
    panel_one, panel_two, sums = finish(near, near_keep, coupling, own, [])
    sums = total_over_all(sums, row_count, col_count, me)
    block_one, block_cross, block_two = close(sums, coupling, diag_first, diag_second)
    return (panel_one, panel_two, block_one, block_cross, block_two)


def solution(mesh):
    return jax.shard_map(
        per_device,
        mesh=mesh,
        in_specs=(
            P("row", "col"),
            P("row", "col"),
            P("col", None),
            P("col", None),
            P(),
            P(),
            P(),
            P(),
            P(),
        ),
        out_specs=(P(AXES, None), P(AXES, None), P(), P(), P()),
        check_vma=False,
    )
```

```python
import functools

import jax
import jax.numpy as jnp
from jax import lax
from jax.experimental import pallas as pl
from jax.experimental.pallas import tpu as pltpu
from jax.sharding import PartitionSpec as P

BLK = 128
K0_MIB = 52
AXES = ("row", "col")
F32 = jnp.float32
BF16 = jnp.bfloat16
ROWS_DIM = (((0,), (0,)), ((), ()))


def halves(value):
    high = value.astype(BF16)
    low = (value - high.astype(F32)).astype(BF16)
    return high, low


def dot3(a, b, dims=(((1,), (0,)), ((), ()))):
    a_high, a_low = halves(a)
    b_high, b_low = halves(b)
    mul = functools.partial(lax.dot_general, dimension_numbers=dims, preferred_element_type=F32)
    return mul(a_high, b_high) + (mul(a_high, b_low) + mul(a_low, b_high))


def kept(value, rows_list, first_block):
    blocks = value.shape[0] // BLK
    ids = first_block + lax.broadcasted_iota(jnp.int32, (blocks, rows_list.shape[1]), 0)
    hits = jnp.sum((ids == rows_list).astype(F32), axis=1, keepdims=True)
    parts = [value[b * BLK : (b + 1) * BLK] * hits[b : b + 1] for b in range(blocks)]
    return jnp.concatenate(parts, axis=0) if blocks > 1 else parts[0]


def collect_slots(info_ref, list_at, count, first_block, blocks, slots_ref, base):
    def collect(i, found):
        block = info_ref[list_at + i] - first_block
        slots_ref[base + found] = block
        here = jnp.logical_and(block >= 0, block < blocks)
        return found + here.astype(jnp.int32)

    found = lax.fori_loop(0, count, collect, 0)
    slots_ref[base + found] = 0
    slots_ref[base + blocks + 1] = found
    return found


def product_body(plan, first, at, info_ref, *rest):
    pieces = len(at)
    if first:
        a_ref, *factors = rest[:3]
        outs, split, slots_ref = rest[3 : 3 + pieces], rest[3 + pieces : 7 + pieces], rest[7 + pieces]
        held, a_sems, staged, sems = rest[8 + pieces :]
    else:
        slots_ref, a_ref = rest[:2]
        split, outs = rest[2:6], rest[6 : 6 + pieces]
        held, a_sems = rest[6 + pieces :]
    tile, depth = held.shape[1:]
    width = split[0].shape[1]
    col_blocks = depth // BLK
    stride = col_blocks + 2
    row_blocks = tile // BLK
    fetches = []
    for p in range(pieces):
        rows = pl.ds(pl.multiple_of(info_ref[at[p]] * tile, tile), tile)
        fetches.append(pltpu.make_async_copy(a_ref.at[rows, :], held.at[p], a_sems.at[p]))
        fetches[p].start()

    if first:
        founds = [
            collect_slots(
                info_ref,
                plan.lists_at + panel * plan.list_size,
                plan.list_size,
                info_ref[plan.block_at],
                col_blocks,
                slots_ref,
                panel * stride,
            )
            for panel in range(2)
        ]

        def stage(panel, slot):
            row = pl.multiple_of(slots_ref[panel * stride + slot] * BLK, BLK)
            source = factors[panel].at[pl.ds(row, BLK), :]
            return pltpu.make_async_copy(source, staged.at[panel, slot], sems.at[panel, slot])

        for panel in range(2):

            @pl.loop(0, (founds[panel] + 1) // 2 * 2)
            def _(slot):
                stage(panel, slot).start()

        for panel in range(2):

            @pl.loop(0, (founds[panel] + 1) // 2 * 2)
            def _(slot):
                stage(panel, slot).wait()
                high, low = halves(staged[panel, slot] * (slot < founds[panel]).astype(F32))
                to = pl.ds(pl.multiple_of(slot * BLK, BLK), BLK)
                split[2 * panel][to, :] = high
                split[2 * panel + 1][to, :] = low

    mul = functools.partial(jnp.dot, preferred_element_type=F32)
    group = min(8, col_blocks)

    for p, out_ref in enumerate(outs):
        row0 = info_ref[at[p]] * row_blocks
        out_ref[...] = jnp.zeros_like(out_ref)
        fetches[p].wait()
        for panel in range(2):
            base = panel * stride
            high_ref, low_ref = split[2 * panel : 2 * panel + 2]
            columns_at = slice(panel * width, (panel + 1) * width)
            pairs = (slots_ref[base + col_blocks + 1] + 1) // 2

            def part(slot, blocks):
                rows = pl.ds(pl.multiple_of(slot * BLK, 2 * BLK), blocks * BLK)
                x_high, x_low = high_ref[rows, :], low_ref[rows, :]
                columns = []
                for s in range(blocks):
                    block = slots_ref[base + slot + s]
                    lanes = pl.ds(pl.multiple_of(block * BLK, BLK), BLK)
                    cells = [
                        held[p, i * BLK : (i + 1) * BLK, lanes]
                        * info_ref[plan.pattern_at + (row0 + i) * col_blocks + block].astype(F32)
                        for i in range(row_blocks)
                    ]
                    columns.append(jnp.concatenate(cells, axis=0) if row_blocks > 1 else cells[0])
                a_high, a_low = halves(jnp.concatenate(columns, axis=1))
                out_ref[:, columns_at] += mul(a_high, x_high)
                out_ref[:, columns_at] += mul(a_high, x_low)
                out_ref[:, columns_at] += mul(a_low, x_high)

            full = pairs // (group // 2)

            @pl.loop(0, full)
            def _(at):
                part(at * group, group)

            for left in range(1, group // 2):

                @pl.when(pairs % (group // 2) == left)
                def _():
                    part(full * group, 2 * left)


def smem():
    return pl.BlockSpec(memory_space=pltpu.SMEM)


def vmem():
    return pl.BlockSpec(memory_space=pltpu.VMEM)


class Plan:
    def __init__(self, places, first_block, lists, pattern):
        self.list_size = lists[0].shape[0]
        parts = [jnp.stack(places + [first_block]).astype(jnp.int32), *lists, pattern.reshape(-1)]
        self.info = jnp.concatenate(parts)
        self.block_at = len(places)
        self.lists_at = self.block_at + 1
        self.pattern_at = self.lists_at + 2 * self.list_size


def product(plan, inverse, at, piece_rows, factors=None, split=None):
    pieces = len(at)
    depth = inverse.shape[1]
    col_blocks = depth // BLK
    first = split is None
    width = factors[0].shape[1] if first else split[0].shape[1]
    hbm = pl.BlockSpec(memory_space=pltpu.HBM)
    outs = [jax.ShapeDtypeStruct((piece_rows, 2 * width), F32)] * pieces
    scratch = [pltpu.VMEM((pieces, piece_rows, depth), F32), pltpu.SemaphoreType.DMA((pieces,))]
    if first:
        operands = [plan.info, inverse, *factors]
        in_specs = [smem(), hbm, hbm, hbm]
        outs += [jax.ShapeDtypeStruct((depth, width), BF16)] * 4
        outs += [jax.ShapeDtypeStruct((2 * (col_blocks + 2),), jnp.int32)]
        scratch += [
            pltpu.VMEM((2, col_blocks, BLK, width), F32),
            pltpu.SemaphoreType.DMA((2, col_blocks)),
        ]
    else:
        operands = [plan.info, split[4], inverse, *split[:4]]
        in_specs = [smem(), smem(), hbm] + [vmem()] * 4
    result = pl.pallas_call(
        functools.partial(product_body, plan, first, at),
        in_specs=in_specs,
        out_specs=[vmem()] * (pieces + 4) + [smem()] if first else [vmem()] * pieces,
        out_shape=outs,
        scratch_shapes=scratch,
        compiler_params=pltpu.CompilerParams(vmem_limit_bytes=(K0_MIB if first else 18) * 2**20),
        cost_estimate=pl.CostEstimate(
            flops=6 * pieces * piece_rows * depth * 2 * width,
            bytes_accessed=4 * pieces * piece_rows * depth,
            transcendentals=0,
        ),
        name="product",
    )(*operands)
    return (result[:pieces], result[pieces:]) if first else result


def pick_body(start_ref, first_ref, second_ref, out_ref, sems):
    rows = pl.ds(pl.multiple_of(start_ref[0], BLK), out_ref.shape[1])
    copies = [
        pltpu.make_async_copy(source.at[rows, :], out_ref.at[p], sems.at[p])
        for p, source in enumerate((first_ref, second_ref))
    ]
    for copy in copies:
        copy.start()
    for copy in copies:
        copy.wait()


def pick(start, rows, first, second):
    hbm = pl.BlockSpec(memory_space=pltpu.HBM)
    return pl.pallas_call(
        pick_body,
        in_specs=[smem(), hbm, hbm],
        out_specs=vmem(),
        out_shape=jax.ShapeDtypeStruct((2, rows, first.shape[1]), F32),
        scratch_shapes=[pltpu.SemaphoreType.DMA((2,))],
        compiler_params=pltpu.CompilerParams(vmem_limit_bytes=58 * 2**20),
        name="pick",
    )(start.astype(jnp.int32).reshape(1), first, second)


def finish_body(at_ref, near_ref, first_ref, second_ref, coupling_ref, *rest):
    *added, one_ref, two_ref, sums_ref = rest
    total = tree_sum([ref[...] for ref in added])
    width = coupling_ref.shape[0]
    one = -total[:, :width]
    two = -(total[:, width:] + dot3(one, coupling_ref[...]))
    one_ref[...] = one
    two_ref[...] = two
    x_one = kept(near_ref[0], first_ref[...], at_ref[0])
    x_two = kept(near_ref[1], second_ref[...], at_ref[0])
    sums_ref[:width] = dot3(x_one, one, ROWS_DIM)
    sums_ref[width : 2 * width] = dot3(one, x_two, ROWS_DIM)
    sums_ref[2 * width :] = dot3(x_two, two, ROWS_DIM)


def finish(block_at, near, rows_first, rows_second, coupling, parts):
    rows = parts[0].shape[0]
    width = coupling.shape[0]
    tall = jax.ShapeDtypeStruct((rows, width), F32)
    return pl.pallas_call(
        finish_body,
        in_specs=[smem()] + [vmem()] * (4 + len(parts)),
        out_shape=[tall, tall, jax.ShapeDtypeStruct((3 * width, width), F32)],
        compiler_params=pltpu.CompilerParams(vmem_limit_bytes=16 * 2**20),
        name="finish",
    )(
        block_at.astype(jnp.int32).reshape(1),
        near,
        rows_first.reshape(1, -1),
        rows_second.reshape(1, -1),
        coupling,
        *parts,
    )


def close_body(sums_ref, coupling_ref, first_ref, second_ref, one_ref, cross_ref, two_ref):
    width = coupling_ref.shape[0]
    coupling = coupling_ref[...]
    one = first_ref[...] - sums_ref[:width]
    cross = -(sums_ref[width : 2 * width] + dot3(one, coupling))
    one_ref[...] = one
    cross_ref[...] = cross
    two_ref[...] = second_ref[...] - sums_ref[2 * width :] - dot3(coupling, cross, ROWS_DIM)


def close(sums, coupling, diag_first, diag_second):
    return pl.pallas_call(
        close_body,
        out_shape=[jax.ShapeDtypeStruct(coupling.shape, F32)] * 3,
        compiler_params=pltpu.CompilerParams(vmem_limit_bytes=16 * 2**20),
        name="close",
    )(sums, coupling, diag_first, diag_second)


def flip(value, count, mask_of):
    return lax.ppermute(value, AXES, [(i, i ^ mask_of(i)) for i in range(count)])


def bits_of(count):
    return count.bit_length() - 1


def tree_sum(parts):
    parts = list(parts)
    while len(parts) > 1:
        pairs = [a + b for a, b in zip(parts[::2], parts[1::2])]
        parts = pairs + parts[2 * len(pairs) :]
    return parts[0]


def after(first, *values):
    got = lax.optimization_barrier((first, *values))
    return got[0], got[1:]


def piece_of(row, col, row_count, col_count):
    per_home = col_count // row_count
    mixed = (col // per_home) ^ row
    piece = 0
    for _ in range(bits_of(row_count)):
        piece = piece * 2 + mixed % 2
        mixed = mixed // 2
    return piece ^ ((col % per_home) % 2) * (row_count // 2)


def per_device(
    inverse,
    pattern,
    factor_first,
    factor_second,
    rows_first,
    rows_second,
    coupling,
    diag_first,
    diag_second,
):
    row_count = lax.axis_size("row")
    col_count = lax.axis_size("col")
    count = row_count * col_count
    row_index = lax.axis_index("row")
    col_index = lax.axis_index("col")
    me = row_index * col_count + col_index
    share_rows = factor_first.shape[0]
    quota_rows = inverse.shape[0] // col_count

    along, across = [], []
    for i in range(count):
        row, col = divmod(i, col_count)
        goal = col * row_count + piece_of(row, col, row_count, col_count)
        between = row * col_count + goal % col_count
        along.append((i, between))
        across.append((between, goal))
    start = piece_of(row_index, col_index, row_count, col_count) * quota_rows
    near = pick(start, quota_rows, factor_first, factor_second)
    near, (pattern,) = after(near, pattern)
    near = lax.ppermute(near, AXES, along)
    near = lax.ppermute(near, AXES, across)

    core = col_index & 1
    spare = bits_of(col_count) - 1
    forward = [2 << bit for bit in range(spare)]
    backward = list(reversed(forward))
    order = sorted(
        range(1 << spare), key=lambda e: -int(format(e, "b").zfill(spare)[::-1] or "0", 2)
    )

    places = []
    for e in order:
        offsets = [
            sum(bit for at, bit in enumerate(line) if e >> at & 1) for line in (forward, backward)
        ]
        for own in (0, 1):
            of_core = core if own else 1 - core
            places.append(
                col_index ^ core ^ of_core ^ jnp.where(of_core == 0, offsets[0], offsets[1])
            )
    plan = Plan(places, col_index * (share_rows // BLK), (rows_first, rows_second), pattern)

    last = len(order) - 1
    groups = [[(0, 0)]]
    for i in range(last + 1):
        groups.append([(i, 1)] + ([(i + 1, 0)] if i < last else []))

    arrived = {e: [] for e in order}
    exchanged = {}
    split = None
    result = None
    for group in groups:
        at = [2 * i + own for i, own in group]
        if split is None:
            outs, split = product(plan, inverse, at, quota_rows, (factor_first, factor_second))
        else:
            outs = product(plan, inverse, at, quota_rows, None, split)
        for (i, own), out in zip(group, outs):
            e = order[i]
            if not own:
                exchanged[e] = flip(out, count, lambda i: 1)
                continue
            if i == last:
                result = [out, exchanged[e]] + arrived[e]
                continue
            out = functools.reduce(jnp.add, [out, exchanged[e]] + arrived[e])
            out, split = after(out, *split)
            bit = bits_of(e & -e)
            got = flip(out, count, lambda i: (backward if i & 1 else forward)[bit])
            arrived[e & (e - 1)].append(got)

    panel_one, panel_two, sums = finish(
        me * (quota_rows // BLK), near, rows_first, rows_second, coupling, result
    )

    def stage(at):
        if at == 0:
            return (me & 1) != 0, lambda i: 1
        one, other = forward[at - 1], backward[at - 1]
        high = jnp.where(core == 0, (col_index & one) != 0, (col_index & other) != 0)
        return high, lambda i: other if i & 1 else one

    for at in range(spare + 1):
        high, mask_of = stage(at)
        half = sums.shape[0] // 2
        mine = jnp.where(high, half, 0)
        kept_part = lax.dynamic_slice_in_dim(sums, mine, half, 0)
        sent = lax.dynamic_slice_in_dim(sums, half - mine, half, 0)
        sums = kept_part + flip(sent, count, mask_of)
    for bit in range(bits_of(row_count)):
        sums = sums + flip(sums, count, lambda i: col_count << bit)
    for at in reversed(range(spare + 1)):
        high, mask_of = stage(at)
        other = flip(sums, count, mask_of)
        sums = jnp.concatenate(
            [jnp.where(high, other, sums), jnp.where(high, sums, other)], axis=0
        )
    block_one, block_cross, block_two = close(sums, coupling, diag_first, diag_second)
    return (panel_one, panel_two, block_one, block_cross, block_two)


def solution(mesh):
    return jax.shard_map(
        per_device,
        mesh=mesh,
        in_specs=(
            P("row", "col"),
            P("row", "col"),
            P("col", None),
            P("col", None),
            P(),
            P(),
            P(),
            P(),
            P(),
        ),
        out_specs=(P(AXES, None), P(AXES, None), P(), P(), P()),
        check_vma=False,
    )
```

```python
import functools

import jax
import jax.numpy as jnp
from jax import lax
from jax.experimental import pallas as pl
from jax.experimental.pallas import tpu as pltpu
from jax.sharding import PartitionSpec as P

BLK = 128
K0_MIB = 48
PICK_MIB = 54
AXES = ("row", "col")
F32 = jnp.float32
BF16 = jnp.bfloat16
ROWS_DIM = (((0,), (0,)), ((), ()))


def halves(value):
    high = value.astype(BF16)
    low = (value - high.astype(F32)).astype(BF16)
    return high, low


def dot3(a, b, dims=(((1,), (0,)), ((), ()))):
    a_high, a_low = halves(a)
    b_high, b_low = halves(b)
    mul = functools.partial(lax.dot_general, dimension_numbers=dims, preferred_element_type=F32)
    return mul(a_high, b_high) + (mul(a_high, b_low) + mul(a_low, b_high))


def kept(value, rows_list, first_block):
    blocks = value.shape[0] // BLK
    ids = first_block + lax.broadcasted_iota(jnp.int32, (blocks, rows_list.shape[1]), 0)
    hits = jnp.sum((ids == rows_list).astype(F32), axis=1, keepdims=True)
    parts = [value[b * BLK : (b + 1) * BLK] * hits[b : b + 1] for b in range(blocks)]
    return jnp.concatenate(parts, axis=0) if blocks > 1 else parts[0]


def collect_slots(info_ref, list_at, count, first_block, blocks, slots_ref, base):
    def collect(i, found):
        block = info_ref[list_at + i] - first_block
        slots_ref[base + found] = block
        here = jnp.logical_and(block >= 0, block < blocks)
        return found + here.astype(jnp.int32)

    found = lax.fori_loop(0, count, collect, 0, unroll=8)
    slots_ref[base + found] = 0
    slots_ref[base + blocks + 1] = found
    return found


def product_body(plan, first, at, info_ref, *rest):
    pieces = len(at)
    if first:
        a_ref, *factors = rest[:3]
        outs, split, slots_ref = rest[3 : 3 + pieces], rest[3 + pieces : 7 + pieces], rest[7 + pieces]
        held, a_sems, staged, sems = rest[8 + pieces :]
    else:
        slots_ref, a_ref = rest[:2]
        split, outs = rest[2:6], rest[6 : 6 + pieces]
        held, a_sems = rest[6 + pieces :]
    tile, depth = held.shape[1:]
    width = split[0].shape[1]
    col_blocks = depth // BLK
    stride = col_blocks + 2
    row_blocks = tile // BLK
    fetches = []
    for p in range(pieces):
        rows = pl.ds(pl.multiple_of(info_ref[at[p]] * tile, tile), tile)
        fetches.append(pltpu.make_async_copy(a_ref.at[rows, :], held.at[p], a_sems.at[p]))
        fetches[p].start()

    if first:
        founds = [
            collect_slots(
                info_ref,
                plan.lists_at + panel * plan.list_size,
                plan.list_size,
                info_ref[plan.block_at],
                col_blocks,
                slots_ref,
                panel * stride,
            )
            for panel in range(2)
        ]

        def stage(panel, slot):
            row = pl.multiple_of(slots_ref[panel * stride + slot] * BLK, BLK)
            source = factors[panel].at[pl.ds(row, BLK), :]
            return pltpu.make_async_copy(source, staged.at[panel, slot], sems.at[panel, slot])

        for panel in range(2):

            @pl.loop(0, (founds[panel] + 1) // 2 * 2)
            def _(slot):
                stage(panel, slot).start()

        for panel in range(2):

            @pl.loop(0, (founds[panel] + 1) // 2 * 2)
            def _(slot):
                stage(panel, slot).wait()
                high, low = halves(staged[panel, slot] * (slot < founds[panel]).astype(F32))
                to = pl.ds(pl.multiple_of(slot * BLK, BLK), BLK)
                split[2 * panel][to, :] = high
                split[2 * panel + 1][to, :] = low

    mul = functools.partial(jnp.dot, preferred_element_type=F32)
    group = min(8, col_blocks)

    for p, out_ref in enumerate(outs):
        row0 = info_ref[at[p]] * row_blocks
        out_ref[...] = jnp.zeros_like(out_ref)
        fetches[p].wait()
        for panel in range(2):
            base = panel * stride
            high_ref, low_ref = split[2 * panel : 2 * panel + 2]
            columns_at = slice(panel * width, (panel + 1) * width)
            pairs = (slots_ref[base + col_blocks + 1] + 1) // 2

            def part(slot, blocks):
                rows = pl.ds(pl.multiple_of(slot * BLK, 2 * BLK), blocks * BLK)
                x_high, x_low = high_ref[rows, :], low_ref[rows, :]
                columns = []
                for s in range(blocks):
                    block = slots_ref[base + slot + s]
                    lanes = pl.ds(pl.multiple_of(block * BLK, BLK), BLK)
                    cells = [
                        held[p, i * BLK : (i + 1) * BLK, lanes]
                        * info_ref[plan.pattern_at + (row0 + i) * col_blocks + block].astype(F32)
                        for i in range(row_blocks)
                    ]
                    columns.append(jnp.concatenate(cells, axis=0) if row_blocks > 1 else cells[0])
                a_high, a_low = halves(jnp.concatenate(columns, axis=1))
                out_ref[:, columns_at] += mul(a_high, x_high)
                out_ref[:, columns_at] += mul(a_high, x_low)
                out_ref[:, columns_at] += mul(a_low, x_high)

            full = pairs // (group // 2)

            @pl.loop(0, full)
            def _(at):
                part(at * group, group)

            for left in range(1, group // 2):

                @pl.when(pairs % (group // 2) == left)
                def _():
                    part(full * group, 2 * left)


def smem():
    return pl.BlockSpec(memory_space=pltpu.SMEM)


def vmem():
    return pl.BlockSpec(memory_space=pltpu.VMEM)


class Plan:
    def __init__(self, places, first_block, lists, pattern):
        self.list_size = lists[0].shape[0]
        parts = [jnp.stack(places + [first_block]).astype(jnp.int32), *lists, pattern.reshape(-1)]
        self.info = jnp.concatenate(parts)
        self.block_at = len(places)
        self.lists_at = self.block_at + 1
        self.pattern_at = self.lists_at + 2 * self.list_size


def product(plan, inverse, at, piece_rows, factors=None, split=None):
    pieces = len(at)
    depth = inverse.shape[1]
    col_blocks = depth // BLK
    first = split is None
    width = factors[0].shape[1] if first else split[0].shape[1]
    hbm = pl.BlockSpec(memory_space=pltpu.HBM)
    outs = [jax.ShapeDtypeStruct((piece_rows, 2 * width), F32)] * pieces
    scratch = [pltpu.VMEM((pieces, piece_rows, depth), F32), pltpu.SemaphoreType.DMA((pieces,))]
    if first:
        operands = [plan.info, inverse, *factors]
        in_specs = [smem(), hbm, hbm, hbm]
        outs += [jax.ShapeDtypeStruct((depth, width), BF16)] * 4
        outs += [jax.ShapeDtypeStruct((2 * (col_blocks + 2),), jnp.int32)]
        scratch += [
            pltpu.VMEM((2, col_blocks, BLK, width), F32),
            pltpu.SemaphoreType.DMA((2, col_blocks)),
        ]
    else:
        operands = [plan.info, split[4], inverse, *split[:4]]
        in_specs = [smem(), smem(), hbm] + [vmem()] * 4
    result = pl.pallas_call(
        functools.partial(product_body, plan, first, at),
        in_specs=in_specs,
        out_specs=[vmem()] * (pieces + 4) + [smem()] if first else [vmem()] * pieces,
        out_shape=outs,
        scratch_shapes=scratch,
        compiler_params=pltpu.CompilerParams(vmem_limit_bytes=(K0_MIB if first else 36) * 2**20),
        cost_estimate=pl.CostEstimate(
            flops=1 * pieces * piece_rows * depth * 2 * width,
            bytes_accessed=pieces * piece_rows * depth,
            transcendentals=0,
        ),
        name="product",
    )(*operands)
    return (result[:pieces], result[pieces:]) if first else result


def pick_body(start_ref, first_ref, second_ref, out_ref, sems):
    rows = pl.ds(pl.multiple_of(start_ref[0], BLK), out_ref.shape[1])
    copies = [
        pltpu.make_async_copy(source.at[rows, :], out_ref.at[p], sems.at[p])
        for p, source in enumerate((first_ref, second_ref))
    ]
    for copy in copies:
        copy.start()
    for copy in copies:
        copy.wait()


def pick(start, rows, first, second):
    hbm = pl.BlockSpec(memory_space=pltpu.HBM)
    return pl.pallas_call(
        pick_body,
        in_specs=[smem(), hbm, hbm],
        out_specs=vmem(),
        out_shape=jax.ShapeDtypeStruct((2, rows, first.shape[1]), F32),
        scratch_shapes=[pltpu.SemaphoreType.DMA((2,))],
        compiler_params=pltpu.CompilerParams(vmem_limit_bytes=PICK_MIB * 2**20),
        name="pick",
    )(start.astype(jnp.int32).reshape(1), first, second)


def finish_body(at_ref, near_ref, first_ref, second_ref, coupling_ref, *rest):
    *added, one_ref, two_ref, sums_ref = rest
    total = tree_sum([ref[...] for ref in added])
    width = coupling_ref.shape[0]
    one = -total[:, :width]
    two = -(total[:, width:] + dot3(one, coupling_ref[...]))
    one_ref[...] = one
    two_ref[...] = two
    x_one = kept(near_ref[0], first_ref[...], at_ref[0])
    x_two = kept(near_ref[1], second_ref[...], at_ref[0])
    sums_ref[:width] = dot3(x_one, one, ROWS_DIM)
    sums_ref[width : 2 * width] = dot3(one, x_two, ROWS_DIM)
    sums_ref[2 * width :] = dot3(x_two, two, ROWS_DIM)


def finish(block_at, near, rows_first, rows_second, coupling, parts):
    rows = parts[0].shape[0]
    width = coupling.shape[0]
    tall = jax.ShapeDtypeStruct((rows, width), F32)
    return pl.pallas_call(
        finish_body,
        in_specs=[smem()] + [vmem()] * (4 + len(parts)),
        out_shape=[tall, tall, jax.ShapeDtypeStruct((3 * width, width), F32)],
        compiler_params=pltpu.CompilerParams(vmem_limit_bytes=16 * 2**20),
        name="finish",
    )(
        block_at.astype(jnp.int32).reshape(1),
        near,
        rows_first.reshape(1, -1),
        rows_second.reshape(1, -1),
        coupling,
        *parts,
    )


def close_body(sums_ref, coupling_ref, first_ref, second_ref, one_ref, cross_ref, two_ref):
    width = coupling_ref.shape[0]
    coupling = coupling_ref[...]
    one = first_ref[...] - sums_ref[:width]
    cross = -(sums_ref[width : 2 * width] + dot3(one, coupling))
    one_ref[...] = one
    cross_ref[...] = cross
    two_ref[...] = second_ref[...] - sums_ref[2 * width :] - dot3(coupling, cross, ROWS_DIM)


def close(sums, coupling, diag_first, diag_second):
    return pl.pallas_call(
        close_body,
        out_shape=[jax.ShapeDtypeStruct(coupling.shape, F32)] * 3,
        compiler_params=pltpu.CompilerParams(vmem_limit_bytes=16 * 2**20),
        name="close",
    )(sums, coupling, diag_first, diag_second)


def flip(value, count, mask_of):
    return lax.ppermute(value, AXES, [(i, i ^ mask_of(i)) for i in range(count)])


def bits_of(count):
    return count.bit_length() - 1


def tree_sum(parts):
    parts = list(parts)
    while len(parts) > 1:
        pairs = [a + b for a, b in zip(parts[::2], parts[1::2])]
        parts = pairs + parts[2 * len(pairs) :]
    return parts[0]


def chosen(place, options):
    value = options[-1]
    for at in range(len(options) - 2, -1, -1):
        value = jnp.where(place == at, options[at], value)
    return value


def after(first, *values):
    got = lax.optimization_barrier((first, *values))
    return got[0], got[1:]


def piece_of(row, col, row_count, col_count):
    per_home = col_count // row_count
    mixed = (col // per_home) ^ row
    piece = 0
    for _ in range(bits_of(row_count)):
        piece = piece * 2 + mixed % 2
        mixed = mixed // 2
    return piece ^ ((col % per_home) % 2) * (row_count // 2)


def per_device(
    inverse,
    pattern,
    factor_first,
    factor_second,
    rows_first,
    rows_second,
    coupling,
    diag_first,
    diag_second,
):
    row_count = lax.axis_size("row")
    col_count = lax.axis_size("col")
    count = row_count * col_count
    row_index = lax.axis_index("row")
    col_index = lax.axis_index("col")
    me = row_index * col_count + col_index
    share_rows = factor_first.shape[0]
    quota_rows = inverse.shape[0] // col_count

    along, across = [], []
    for i in range(count):
        row, col = divmod(i, col_count)
        goal = col * row_count + piece_of(row, col, row_count, col_count)
        between = row * col_count + goal % col_count
        along.append((i, between))
        across.append((between, goal))
    start = piece_of(row_index, col_index, row_count, col_count) * quota_rows
    near = pick(start, quota_rows, factor_first, factor_second)
    near, (pattern,) = after(near, pattern)
    near = lax.ppermute(near, AXES, along)

    core = col_index & 1
    spare = bits_of(col_count) - 1
    forward = [2 << bit for bit in range(spare)]
    backward = list(reversed(forward))
    order = sorted(
        range(1 << spare), key=lambda e: -int(format(e, "b").zfill(spare)[::-1] or "0", 2)
    )

    places = []
    for e in order:
        offsets = [
            sum(bit for at, bit in enumerate(line) if e >> at & 1) for line in (forward, backward)
        ]
        for own in (0, 1):
            of_core = core if own else 1 - core
            places.append(
                col_index ^ core ^ of_core ^ jnp.where(of_core == 0, offsets[0], offsets[1])
            )
    plan = Plan(places, col_index * (share_rows // BLK), (rows_first, rows_second), pattern)

    last = len(order) - 1
    groups = [[(0, 0)]]
    for i in range(last - 1):
        groups.append([(i, 1), (i + 1, 0)])
    groups += [[(last - 1, 1)], [(last, 0)], [(last, 1)]]

    arrived = {e: [] for e in order}
    exchanged = {}
    split = None
    result = None
    for turn, group in enumerate(groups):
        if turn == len(groups) - 3:
            near, split = after(near, *split)
            near = lax.ppermute(near, AXES, across)
        at = [2 * i + own for i, own in group]
        if split is None:
            outs, split = product(plan, inverse, at, quota_rows, (factor_first, factor_second))
        else:
            outs = product(plan, inverse, at, quota_rows, None, split)
        for (i, own), out in zip(group, outs):
            e = order[i]
            if not own:
                exchanged[e] = flip(out, count, lambda i: 1)
                continue
            if i == last:
                result = [out, exchanged[e]] + arrived[e]
                continue
            out = functools.reduce(jnp.add, [out, exchanged[e]] + arrived[e])
            out, split = after(out, *split)
            bit = bits_of(e & -e)
            got = flip(out, count, lambda i: (backward if i & 1 else forward)[bit])
            arrived[e & (e - 1)].append(got)

    panel_one, panel_two, sums = finish(
        me * (quota_rows // BLK), near, rows_first, rows_second, coupling, result
    )

    digits = [(1, 2), (2, col_count // 2)]
    for stride, size in digits:
        spot = (me // stride) % size
        part = sums.shape[0] // size
        got = [lax.dynamic_slice_in_dim(sums, spot * part, part, 0)]
        for d in range(1, size):
            sent = lax.dynamic_slice_in_dim(sums, (spot ^ d) * part, part, 0)
            got.append(flip(sent, count, lambda i: d * stride))
        sums = tree_sum(got)
    for bit in range(bits_of(row_count)):
        sums = sums + flip(sums, count, lambda i: col_count << bit)
    for stride, size in reversed(digits):
        spot = (me // stride) % size
        got = [sums] + [flip(sums, count, lambda i: d * stride) for d in range(1, size)]
        sums = jnp.concatenate(
            [chosen(spot, [got[p ^ slot] for p in range(size)]) for slot in range(size)], axis=0
        )
    block_one, block_cross, block_two = close(sums, coupling, diag_first, diag_second)
    return (panel_one, panel_two, block_one, block_cross, block_two)


def solution(mesh):
    return jax.shard_map(
        per_device,
        mesh=mesh,
        in_specs=(
            P("row", "col"),
            P("row", "col"),
            P("col", None),
            P("col", None),
            P(),
            P(),
            P(),
            P(),
            P(),
        ),
        out_specs=(P(AXES, None), P(AXES, None), P(), P(), P()),
        check_vma=False,
    )
```

```python
import functools

import jax
import jax.numpy as jnp
from jax import lax
from jax.experimental import pallas as pl
from jax.experimental.pallas import tpu as pltpu
from jax.sharding import PartitionSpec as P

BLK = 128
COST_FIRST = 1
COST_REST = 1
K0_MIB = 48
PICK_MIB = 54
AXES = ("row", "col")
F32 = jnp.float32
BF16 = jnp.bfloat16
ROWS_DIM = (((0,), (0,)), ((), ()))


def halves(value):
    high = value.astype(BF16)
    low = (value - high.astype(F32)).astype(BF16)
    return high, low


def dot3(a, b, dims=(((1,), (0,)), ((), ()))):
    a_high, a_low = halves(a)
    b_high, b_low = halves(b)
    mul = functools.partial(lax.dot_general, dimension_numbers=dims, preferred_element_type=F32)
    return mul(a_high, b_high) + (mul(a_high, b_low) + mul(a_low, b_high))


def kept(value, rows_list, first_block):
    blocks = value.shape[0] // BLK
    ids = first_block + lax.broadcasted_iota(jnp.int32, (blocks, rows_list.shape[1]), 0)
    hits = jnp.sum((ids == rows_list).astype(F32), axis=1, keepdims=True)
    parts = [value[b * BLK : (b + 1) * BLK] * hits[b : b + 1] for b in range(blocks)]
    return jnp.concatenate(parts, axis=0) if blocks > 1 else parts[0]


def collect_slots(info_ref, list_at, count, first_block, blocks, slots_ref, base):
    def collect(i, found):
        block = info_ref[list_at + i] - first_block
        slots_ref[base + found] = block
        here = jnp.logical_and(block >= 0, block < blocks)
        return found + here.astype(jnp.int32)

    found = lax.fori_loop(0, count, collect, 0, unroll=8)
    slots_ref[base + found] = 0
    slots_ref[base + blocks + 1] = found
    return found


def product_body(plan, first, at, info_ref, *rest):
    pieces = len(at)
    if first:
        a_ref, *factors = rest[:3]
        outs, (high_ref, low_ref, slots_ref) = rest[3 : 3 + pieces], rest[3 + pieces : 6 + pieces]
        held, a_sems, sum_ref, staged, sems = rest[6 + pieces :]
    else:
        slots_ref, a_ref, high_ref, low_ref = rest[:4]
        outs = rest[4 : 4 + pieces]
        held, a_sems, sum_ref = rest[4 + pieces :]
    tile, depth = held.shape[1:]
    width = high_ref.shape[1]
    col_blocks = depth // BLK
    stride = col_blocks + 2
    row_blocks = tile // BLK

    def place_of(piece):
        place = info_ref[at[0]]
        for p in range(1, pieces):
            place = jnp.where(piece == p, info_ref[at[p]], place)
        return place

    def fetch(piece):
        rows = pl.ds(pl.multiple_of(place_of(piece) * tile, tile), tile)
        return pltpu.make_async_copy(a_ref.at[rows, :], held.at[piece], a_sems.at[piece])

    for p in range(pieces):
        fetch(p).start()

    if first:
        founds = [
            collect_slots(
                info_ref,
                plan.lists_at + panel * plan.list_size,
                plan.list_size,
                info_ref[plan.block_at],
                col_blocks,
                slots_ref,
                panel * stride,
            )
            for panel in range(2)
        ]

        def stage(panel, slot):
            row = pl.multiple_of(slots_ref[panel * stride + slot] * BLK, BLK)
            source = factors[panel].at[pl.ds(row, BLK), :]
            return pltpu.make_async_copy(source, staged.at[panel, slot], sems.at[panel, slot])

        for panel in range(2):

            @pl.loop(0, (founds[panel] + 1) // 2 * 2)
            def _(slot):
                stage(panel, slot).start()

        for panel in range(2):

            @pl.loop(0, (founds[panel] + 1) // 2 * 2)
            def _(slot):
                stage(panel, slot).wait()
                high, low = halves(staged[panel, slot] * (slot < founds[panel]).astype(F32))
                to = pl.ds(pl.multiple_of(panel * depth + slot * BLK, BLK), BLK)
                high_ref[to, :] = high
                low_ref[to, :] = low

    mul = functools.partial(jnp.dot, preferred_element_type=F32)
    group = min(8, col_blocks)

    @pl.loop(0, 2 * pieces)
    def _(turn):
        piece = turn // 2
        panel = turn % 2

        @pl.when(panel == 0)
        def _():
            fetch(piece).wait()

        row0 = place_of(piece) * row_blocks
        base = panel * stride
        columns_at = pl.ds(pl.multiple_of(panel * width, width), width)
        pairs = (slots_ref[base + col_blocks + 1] + 1) // 2
        sum_ref[:, columns_at] = jnp.zeros((tile, width), F32)

        def part(slot, blocks):
            rows = pl.ds(pl.multiple_of(panel * depth + slot * BLK, 2 * BLK), blocks * BLK)
            x_high, x_low = high_ref[rows, :], low_ref[rows, :]
            columns = []
            for s in range(blocks):
                block = slots_ref[base + slot + s]
                lanes = pl.ds(pl.multiple_of(block * BLK, BLK), BLK)
                cells = [
                    held[piece, i * BLK : (i + 1) * BLK, lanes]
                    * info_ref[plan.pattern_at + (row0 + i) * col_blocks + block].astype(F32)
                    for i in range(row_blocks)
                ]
                columns.append(jnp.concatenate(cells, axis=0) if row_blocks > 1 else cells[0])
            a_high, a_low = halves(jnp.concatenate(columns, axis=1))
            sum_ref[:, columns_at] += mul(a_high, x_high)
            sum_ref[:, columns_at] += mul(a_high, x_low)
            sum_ref[:, columns_at] += mul(a_low, x_high)

        whole = [n for n in (5, 6) if group // 2 < n <= col_blocks // 2]
        split_up = jnp.bool_(True)
        for n in whole:
            split_up = jnp.logical_and(split_up, pairs != n)
        full = jnp.where(split_up, pairs // (group // 2), 0)

        @pl.loop(0, full)
        def _(at):
            part(at * group, group)

        for left in range(1, group // 2):

            @pl.when(jnp.logical_and(split_up, pairs % (group // 2) == left))
            def _():
                part(full * group, 2 * left)

        for n in whole:

            @pl.when(pairs == n)
            def _():
                part(0, 2 * n)

        for p, out_ref in enumerate(outs):

            @pl.when(turn == 2 * p + 1)
            def _():
                out_ref[...] = sum_ref[...]


def smem():
    return pl.BlockSpec(memory_space=pltpu.SMEM)


def vmem():
    return pl.BlockSpec(memory_space=pltpu.VMEM)


class Plan:
    def __init__(self, places, first_block, lists, pattern):
        self.list_size = lists[0].shape[0]
        parts = [jnp.stack(places + [first_block]).astype(jnp.int32), *lists, pattern.reshape(-1)]
        self.info = jnp.concatenate(parts)
        self.block_at = len(places)
        self.lists_at = self.block_at + 1
        self.pattern_at = self.lists_at + 2 * self.list_size


def product(plan, inverse, at, piece_rows, factors=None, split=None):
    pieces = len(at)
    depth = inverse.shape[1]
    col_blocks = depth // BLK
    first = split is None
    width = factors[0].shape[1] if first else split[0].shape[1]
    hbm = pl.BlockSpec(memory_space=pltpu.HBM)
    outs = [jax.ShapeDtypeStruct((piece_rows, 2 * width), F32)] * pieces
    scratch = [pltpu.VMEM((pieces, piece_rows, depth), F32), pltpu.SemaphoreType.DMA((pieces,))]
    scratch += [pltpu.VMEM((piece_rows, 2 * width), F32)]
    if first:
        operands = [plan.info, inverse, *factors]
        in_specs = [smem(), hbm, hbm, hbm]
        outs += [jax.ShapeDtypeStruct((2 * depth, width), BF16)] * 2
        outs += [jax.ShapeDtypeStruct((2 * (col_blocks + 2),), jnp.int32)]
        scratch += [
            pltpu.VMEM((2, col_blocks, BLK, width), F32),
            pltpu.SemaphoreType.DMA((2, col_blocks)),
        ]
    else:
        operands = [plan.info, split[2], inverse, *split[:2]]
        in_specs = [smem(), smem(), hbm] + [vmem()] * 2
    result = pl.pallas_call(
        functools.partial(product_body, plan, first, at),
        in_specs=in_specs,
        out_specs=[vmem()] * (pieces + 2) + [smem()] if first else [vmem()] * pieces,
        out_shape=outs,
        scratch_shapes=scratch,
        compiler_params=pltpu.CompilerParams(vmem_limit_bytes=(K0_MIB if first else 36) * 2**20),
        cost_estimate=pl.CostEstimate(
            flops=(COST_FIRST if first else COST_REST) * pieces * piece_rows * depth * 2 * width,
            bytes_accessed=pieces * piece_rows * depth,
            transcendentals=0,
        ),
        name="product",
    )(*operands)
    return (result[:pieces], result[pieces:]) if first else result


def pick_body(start_ref, first_ref, second_ref, out_ref, sems):
    rows = pl.ds(pl.multiple_of(start_ref[0], BLK), out_ref.shape[1])
    copies = [
        pltpu.make_async_copy(source.at[rows, :], out_ref.at[p], sems.at[p])
        for p, source in enumerate((first_ref, second_ref))
    ]
    for copy in copies:
        copy.start()
    for copy in copies:
        copy.wait()


def pick(start, rows, first, second):
    hbm = pl.BlockSpec(memory_space=pltpu.HBM)
    return pl.pallas_call(
        pick_body,
        in_specs=[smem(), hbm, hbm],
        out_specs=vmem(),
        out_shape=jax.ShapeDtypeStruct((2, rows, first.shape[1]), F32),
        scratch_shapes=[pltpu.SemaphoreType.DMA((2,))],
        compiler_params=pltpu.CompilerParams(vmem_limit_bytes=PICK_MIB * 2**20),
        name="pick",
    )(start.astype(jnp.int32).reshape(1), first, second)


def finish_body(at_ref, near_ref, first_ref, second_ref, coupling_ref, *rest):
    *added, one_ref, two_ref, sums_ref = rest
    total = tree_sum([ref[...] for ref in added])
    width = coupling_ref.shape[0]
    one = -total[:, :width]
    two = -(total[:, width:] + dot3(one, coupling_ref[...]))
    one_ref[...] = one
    two_ref[...] = two
    x_one = kept(near_ref[0], first_ref[...], at_ref[0])
    x_two = kept(near_ref[1], second_ref[...], at_ref[0])
    sums_ref[:width] = dot3(x_one, one, ROWS_DIM)
    sums_ref[width : 2 * width] = dot3(one, x_two, ROWS_DIM)
    sums_ref[2 * width :] = dot3(x_two, two, ROWS_DIM)


def finish(block_at, near, rows_first, rows_second, coupling, parts):
    rows = parts[0].shape[0]
    width = coupling.shape[0]
    tall = jax.ShapeDtypeStruct((rows, width), F32)
    return pl.pallas_call(
        finish_body,
        in_specs=[smem()] + [vmem()] * (4 + len(parts)),
        out_shape=[tall, tall, jax.ShapeDtypeStruct((3 * width, width), F32)],
        compiler_params=pltpu.CompilerParams(vmem_limit_bytes=16 * 2**20),
        name="finish",
    )(
        block_at.astype(jnp.int32).reshape(1),
        near,
        rows_first.reshape(1, -1),
        rows_second.reshape(1, -1),
        coupling,
        *parts,
    )


def close_body(sums_ref, coupling_ref, first_ref, second_ref, one_ref, cross_ref, two_ref):
    width = coupling_ref.shape[0]
    coupling = coupling_ref[...]
    one = first_ref[...] - sums_ref[:width]
    cross = -(sums_ref[width : 2 * width] + dot3(one, coupling))
    one_ref[...] = one
    cross_ref[...] = cross
    two_ref[...] = second_ref[...] - sums_ref[2 * width :] - dot3(coupling, cross, ROWS_DIM)


def close(sums, coupling, diag_first, diag_second):
    return pl.pallas_call(
        close_body,
        out_shape=[jax.ShapeDtypeStruct(coupling.shape, F32)] * 3,
        compiler_params=pltpu.CompilerParams(vmem_limit_bytes=16 * 2**20),
        name="close",
    )(sums, coupling, diag_first, diag_second)


def flip(value, count, mask_of):
    return lax.ppermute(value, AXES, [(i, i ^ mask_of(i)) for i in range(count)])


def bits_of(count):
    return count.bit_length() - 1


def tree_sum(parts):
    parts = list(parts)
    while len(parts) > 1:
        pairs = [a + b for a, b in zip(parts[::2], parts[1::2])]
        parts = pairs + parts[2 * len(pairs) :]
    return parts[0]


def chosen(place, options):
    value = options[-1]
    for at in range(len(options) - 2, -1, -1):
        value = jnp.where(place == at, options[at], value)
    return value


def after(first, *values):
    got = lax.optimization_barrier((first, *values))
    return got[0], got[1:]


def piece_of(row, col, row_count, col_count):
    per_home = col_count // row_count
    mixed = (col // per_home) ^ row
    piece = 0
    for _ in range(bits_of(row_count)):
        piece = piece * 2 + mixed % 2
        mixed = mixed // 2
    return piece ^ ((col % per_home) % 2) * (row_count // 2)


def per_device(
    inverse,
    pattern,
    factor_first,
    factor_second,
    rows_first,
    rows_second,
    coupling,
    diag_first,
    diag_second,
):
    row_count = lax.axis_size("row")
    col_count = lax.axis_size("col")
    count = row_count * col_count
    row_index = lax.axis_index("row")
    col_index = lax.axis_index("col")
    me = row_index * col_count + col_index
    share_rows = factor_first.shape[0]
    quota_rows = inverse.shape[0] // col_count

    along, across = [], []
    for i in range(count):
        row, col = divmod(i, col_count)
        goal = col * row_count + piece_of(row, col, row_count, col_count)
        between = row * col_count + goal % col_count
        along.append((i, between))
        across.append((between, goal))
    start = piece_of(row_index, col_index, row_count, col_count) * quota_rows
    near = pick(start, quota_rows, factor_first, factor_second)
    near, (pattern,) = after(near, pattern)
    near = lax.ppermute(near, AXES, along)

    core = col_index & 1
    spare = bits_of(col_count) - 1
    forward = [2 << bit for bit in range(spare)]
    backward = list(reversed(forward))
    order = sorted(
        range(1 << spare), key=lambda e: -int(format(e, "b").zfill(spare)[::-1] or "0", 2)
    )

    places = []
    for e in order:
        offsets = [
            sum(bit for at, bit in enumerate(line) if e >> at & 1) for line in (forward, backward)
        ]
        for own in (0, 1):
            of_core = core if own else 1 - core
            places.append(
                col_index ^ core ^ of_core ^ jnp.where(of_core == 0, offsets[0], offsets[1])
            )
    plan = Plan(places, col_index * (share_rows // BLK), (rows_first, rows_second), pattern)

    last = len(order) - 1
    groups = [[(0, 0)]]
    for i in range(last - 1):
        groups.append([(i, 1), (i + 1, 0)])
    groups += [[(last - 1, 1)], [(last, 0)], [(last, 1)]]

    arrived = {e: [] for e in order}
    exchanged = {}
    split = None
    result = None
    for turn, group in enumerate(groups):
        if turn == len(groups) - 3:
            near, split = after(near, *split)
            near = lax.ppermute(near, AXES, across)
        at = [2 * i + own for i, own in group]
        if split is None:
            outs, split = product(plan, inverse, at, quota_rows, (factor_first, factor_second))
        else:
            outs = product(plan, inverse, at, quota_rows, None, split)
        for (i, own), out in zip(group, outs):
            e = order[i]
            if not own:
                exchanged[e] = flip(out, count, lambda i: 1)
                continue
            if i == last:
                result = [out, exchanged[e]] + arrived[e]
                continue
            out = functools.reduce(jnp.add, [out, exchanged[e]] + arrived[e])
            out, split = after(out, *split)
            bit = bits_of(e & -e)
            got = flip(out, count, lambda i: (backward if i & 1 else forward)[bit])
            arrived[e & (e - 1)].append(got)

    panel_one, panel_two, sums = finish(
        me * (quota_rows // BLK), near, rows_first, rows_second, coupling, result
    )

    digits = [(1, 2), (2, col_count // 2)]
    for stride, size in digits:
        spot = (me // stride) % size
        part = sums.shape[0] // size
        got = [lax.dynamic_slice_in_dim(sums, spot * part, part, 0)]
        for d in range(1, size):
            sent = lax.dynamic_slice_in_dim(sums, (spot ^ d) * part, part, 0)
            got.append(flip(sent, count, lambda i: d * stride))
        sums = tree_sum(got)
    for bit in range(bits_of(row_count)):
        sums = sums + flip(sums, count, lambda i: col_count << bit)
    for stride, size in reversed(digits):
        spot = (me // stride) % size
        got = [sums] + [flip(sums, count, lambda i: d * stride) for d in range(1, size)]
        sums = jnp.concatenate(
            [chosen(spot, [got[p ^ slot] for p in range(size)]) for slot in range(size)], axis=0
        )
    block_one, block_cross, block_two = close(sums, coupling, diag_first, diag_second)
    return (panel_one, panel_two, block_one, block_cross, block_two)


def solution(mesh):
    return jax.shard_map(
        per_device,
        mesh=mesh,
        in_specs=(
            P("row", "col"),
            P("row", "col"),
            P("col", None),
            P("col", None),
            P(),
            P(),
            P(),
            P(),
            P(),
        ),
        out_specs=(P(AXES, None), P(AXES, None), P(), P(), P()),
        check_vma=False,
    )
```

```python
import functools

import jax
import jax.numpy as jnp
from jax import lax
from jax.experimental import pallas as pl
from jax.experimental.pallas import tpu as pltpu
from jax.sharding import PartitionSpec as P

BLK = 128
COST_FIRST = 1
COST_REST = 1
K0_MIB = 48
PICK_MIB = 54
AXES = ("row", "col")
F32 = jnp.float32
BF16 = jnp.bfloat16
ROWS_DIM = (((0,), (0,)), ((), ()))


def halves(value):
    high = value.astype(BF16)
    low = (value - high.astype(F32)).astype(BF16)
    return high, low


def dot3(a, b, dims=(((1,), (0,)), ((), ()))):
    a_high, a_low = halves(a)
    b_high, b_low = halves(b)
    mul = functools.partial(lax.dot_general, dimension_numbers=dims, preferred_element_type=F32)
    return mul(a_high, b_high) + (mul(a_high, b_low) + mul(a_low, b_high))


def kept(value, rows_list, first_block):
    blocks = value.shape[0] // BLK
    ids = first_block + lax.broadcasted_iota(jnp.int32, (blocks, rows_list.shape[1]), 0)
    hits = jnp.sum((ids == rows_list).astype(F32), axis=1, keepdims=True)
    parts = [value[b * BLK : (b + 1) * BLK] * hits[b : b + 1] for b in range(blocks)]
    return jnp.concatenate(parts, axis=0) if blocks > 1 else parts[0]


def collect_slots(info_ref, list_at, count, first_block, blocks, slots_ref, base):
    def collect(i, found):
        block = info_ref[list_at + i] - first_block
        slots_ref[base + found] = block
        here = jnp.logical_and(block >= 0, block < blocks)
        return found + here.astype(jnp.int32)

    found = lax.fori_loop(0, count, collect, 0, unroll=8)
    slots_ref[base + found] = 0
    slots_ref[base + blocks + 1] = found
    return found


def product_body(plan, first, at, info_ref, *rest):
    pieces = len(at)
    if first:
        a_ref, *factors = rest[:3]
        outs, (high_ref, low_ref, slots_ref) = rest[3 : 3 + pieces], rest[3 + pieces : 6 + pieces]
        held, a_sems, sum_ref, staged, sems = rest[6 + pieces :]
    else:
        slots_ref, a_ref, high_ref, low_ref = rest[:4]
        outs = rest[4 : 4 + pieces]
        held, a_sems, sum_ref = rest[4 + pieces :]
    tile, depth = held.shape[1:]
    width = high_ref.shape[1]
    col_blocks = depth // BLK
    stride = col_blocks + 2
    row_blocks = tile // BLK

    def place_of(piece):
        place = info_ref[at[0]]
        for p in range(1, pieces):
            place = jnp.where(piece == p, info_ref[at[p]], place)
        return place

    def fetch(piece):
        rows = pl.ds(pl.multiple_of(place_of(piece) * tile, tile), tile)
        return pltpu.make_async_copy(a_ref.at[rows, :], held.at[piece], a_sems.at[piece])

    for p in range(pieces):
        fetch(p).start()

    if first:
        founds = [
            collect_slots(
                info_ref,
                plan.lists_at + panel * plan.list_size,
                plan.list_size,
                info_ref[plan.block_at],
                col_blocks,
                slots_ref,
                panel * stride,
            )
            for panel in range(2)
        ]

        def stage(panel, slot):
            row = pl.multiple_of(slots_ref[panel * stride + slot] * BLK, BLK)
            source = factors[panel].at[pl.ds(row, BLK), :]
            return pltpu.make_async_copy(source, staged.at[panel, slot], sems.at[panel, slot])

        for panel in range(2):

            @pl.loop(0, (founds[panel] + 1) // 2 * 2)
            def _(slot):
                stage(panel, slot).start()

        for panel in range(2):

            @pl.loop(0, (founds[panel] + 1) // 2 * 2)
            def _(slot):
                stage(panel, slot).wait()
                high, low = halves(staged[panel, slot] * (slot < founds[panel]).astype(F32))
                to = pl.ds(pl.multiple_of(panel * depth + slot * BLK, BLK), BLK)
                high_ref[to, :] = high
                low_ref[to, :] = low

    mul = functools.partial(jnp.dot, preferred_element_type=F32)
    group = min(8, col_blocks)

    @pl.loop(0, 2 * pieces)
    def _(turn):
        piece = turn // 2
        panel = turn % 2

        @pl.when(panel == 0)
        def _():
            fetch(piece).wait()

        row0 = place_of(piece) * row_blocks
        base = panel * stride
        columns_at = pl.ds(pl.multiple_of(panel * width, width), width)
        pairs = (slots_ref[base + col_blocks + 1] + 1) // 2
        sum_ref[:, columns_at] = jnp.zeros((tile, width), F32)

        def part(slot, blocks):
            rows = pl.ds(pl.multiple_of(panel * depth + slot * BLK, 2 * BLK), blocks * BLK)
            x_high, x_low = high_ref[rows, :], low_ref[rows, :]
            columns = []
            for s in range(blocks):
                block = slots_ref[base + slot + s]
                lanes = pl.ds(pl.multiple_of(block * BLK, BLK), BLK)
                cells = [
                    held[piece, i * BLK : (i + 1) * BLK, lanes]
                    * info_ref[plan.pattern_at + (row0 + i) * col_blocks + block].astype(F32)
                    for i in range(row_blocks)
                ]
                columns.append(jnp.concatenate(cells, axis=0) if row_blocks > 1 else cells[0])
            a_high, a_low = halves(jnp.concatenate(columns, axis=1))
            sum_ref[:, columns_at] += mul(a_high, x_high)
            sum_ref[:, columns_at] += mul(a_high, x_low)
            sum_ref[:, columns_at] += mul(a_low, x_high)

        whole = [n for n in (5, 6, 7) if group // 2 < n <= col_blocks // 2]
        split_up = jnp.bool_(True)
        for n in whole:
            split_up = jnp.logical_and(split_up, pairs != n)
        full = jnp.where(split_up, pairs // (group // 2), 0)

        @pl.loop(0, full)
        def _(at):
            part(at * group, group)

        for left in range(1, group // 2):

            @pl.when(jnp.logical_and(split_up, pairs % (group // 2) == left))
            def _():
                part(full * group, 2 * left)

        for n in whole:

            @pl.when(pairs == n)
            def _():
                part(0, 2 * n)

        for p, out_ref in enumerate(outs):

            @pl.when(turn == 2 * p + 1)
            def _():
                out_ref[...] = sum_ref[...]


def smem():
    return pl.BlockSpec(memory_space=pltpu.SMEM)


def vmem():
    return pl.BlockSpec(memory_space=pltpu.VMEM)


class Plan:
    def __init__(self, places, first_block, lists, pattern):
        self.list_size = lists[0].shape[0]
        parts = [jnp.stack(places + [first_block]).astype(jnp.int32), *lists, pattern.reshape(-1)]
        self.info = jnp.concatenate(parts)
        self.block_at = len(places)
        self.lists_at = self.block_at + 1
        self.pattern_at = self.lists_at + 2 * self.list_size


def product(plan, inverse, at, piece_rows, factors=None, split=None):
    pieces = len(at)
    depth = inverse.shape[1]
    col_blocks = depth // BLK
    first = split is None
    width = factors[0].shape[1] if first else split[0].shape[1]
    hbm = pl.BlockSpec(memory_space=pltpu.HBM)
    outs = [jax.ShapeDtypeStruct((piece_rows, 2 * width), F32)] * pieces
    scratch = [pltpu.VMEM((pieces, piece_rows, depth), F32), pltpu.SemaphoreType.DMA((pieces,))]
    scratch += [pltpu.VMEM((piece_rows, 2 * width), F32)]
    if first:
        operands = [plan.info, inverse, *factors]
        in_specs = [smem(), hbm, hbm, hbm]
        outs += [jax.ShapeDtypeStruct((2 * depth, width), BF16)] * 2
        outs += [jax.ShapeDtypeStruct((2 * (col_blocks + 2),), jnp.int32)]
        scratch += [
            pltpu.VMEM((2, col_blocks, BLK, width), F32),
            pltpu.SemaphoreType.DMA((2, col_blocks)),
        ]
    else:
        operands = [plan.info, split[2], inverse, *split[:2]]
        in_specs = [smem(), smem(), hbm] + [vmem()] * 2
    result = pl.pallas_call(
        functools.partial(product_body, plan, first, at),
        in_specs=in_specs,
        out_specs=[vmem()] * (pieces + 2) + [smem()] if first else [vmem()] * pieces,
        out_shape=outs,
        scratch_shapes=scratch,
        compiler_params=pltpu.CompilerParams(vmem_limit_bytes=(K0_MIB if first else 36) * 2**20),
        cost_estimate=pl.CostEstimate(
            flops=(COST_FIRST if first else COST_REST) * pieces * piece_rows * depth * 2 * width,
            bytes_accessed=pieces * piece_rows * depth,
            transcendentals=0,
        ),
        name="product",
    )(*operands)
    return (result[:pieces], result[pieces:]) if first else result


def pick_body(start_ref, first_ref, second_ref, out_ref, sems):
    rows = pl.ds(pl.multiple_of(start_ref[0], BLK), out_ref.shape[1])
    copies = [
        pltpu.make_async_copy(source.at[rows, :], out_ref.at[p], sems.at[p])
        for p, source in enumerate((first_ref, second_ref))
    ]
    for copy in copies:
        copy.start()
    for copy in copies:
        copy.wait()


def pick(start, rows, first, second):
    hbm = pl.BlockSpec(memory_space=pltpu.HBM)
    return pl.pallas_call(
        pick_body,
        in_specs=[smem(), hbm, hbm],
        out_specs=vmem(),
        out_shape=jax.ShapeDtypeStruct((2, rows, first.shape[1]), F32),
        scratch_shapes=[pltpu.SemaphoreType.DMA((2,))],
        compiler_params=pltpu.CompilerParams(vmem_limit_bytes=PICK_MIB * 2**20),
        name="pick",
    )(start.astype(jnp.int32).reshape(1), first, second)


def finish_body(at_ref, near_ref, first_ref, second_ref, coupling_ref, *rest):
    *added, one_ref, two_ref, sums_ref = rest
    total = tree_sum([ref[...] for ref in added])
    width = coupling_ref.shape[0]
    one = -total[:, :width]
    two = -(total[:, width:] + dot3(one, coupling_ref[...]))
    one_ref[...] = one
    two_ref[...] = two
    x_one = kept(near_ref[0], first_ref[...], at_ref[0])
    x_two = kept(near_ref[1], second_ref[...], at_ref[0])
    sums_ref[:width] = dot3(x_one, one, ROWS_DIM)
    sums_ref[width : 2 * width] = dot3(one, x_two, ROWS_DIM)
    sums_ref[2 * width :] = dot3(x_two, two, ROWS_DIM)


def finish(block_at, near, rows_first, rows_second, coupling, parts):
    rows = parts[0].shape[0]
    width = coupling.shape[0]
    tall = jax.ShapeDtypeStruct((rows, width), F32)
    return pl.pallas_call(
        finish_body,
        in_specs=[smem()] + [vmem()] * (4 + len(parts)),
        out_shape=[tall, tall, jax.ShapeDtypeStruct((3 * width, width), F32)],
        compiler_params=pltpu.CompilerParams(vmem_limit_bytes=16 * 2**20),
        name="finish",
    )(
        block_at.astype(jnp.int32).reshape(1),
        near,
        rows_first.reshape(1, -1),
        rows_second.reshape(1, -1),
        coupling,
        *parts,
    )


def close_body(sums_ref, coupling_ref, first_ref, second_ref, one_ref, cross_ref, two_ref):
    width = coupling_ref.shape[0]
    coupling = coupling_ref[...]
    one = first_ref[...] - sums_ref[:width]
    cross = -(sums_ref[width : 2 * width] + dot3(one, coupling))
    one_ref[...] = one
    cross_ref[...] = cross
    two_ref[...] = second_ref[...] - sums_ref[2 * width :] - dot3(coupling, cross, ROWS_DIM)


def close(sums, coupling, diag_first, diag_second):
    return pl.pallas_call(
        close_body,
        out_shape=[jax.ShapeDtypeStruct(coupling.shape, F32)] * 3,
        compiler_params=pltpu.CompilerParams(vmem_limit_bytes=16 * 2**20),
        name="close",
    )(sums, coupling, diag_first, diag_second)


def flip(value, count, mask_of):
    return lax.ppermute(value, AXES, [(i, i ^ mask_of(i)) for i in range(count)])


def bits_of(count):
    return count.bit_length() - 1


def tree_sum(parts):
    parts = list(parts)
    while len(parts) > 1:
        pairs = [a + b for a, b in zip(parts[::2], parts[1::2])]
        parts = pairs + parts[2 * len(pairs) :]
    return parts[0]


def chosen(place, options):
    value = options[-1]
    for at in range(len(options) - 2, -1, -1):
        value = jnp.where(place == at, options[at], value)
    return value


def after(first, *values):
    got = lax.optimization_barrier((first, *values))
    return got[0], got[1:]


def piece_of(row, col, row_count, col_count):
    per_home = col_count // row_count
    mixed = (col // per_home) ^ row
    piece = 0
    for _ in range(bits_of(row_count)):
        piece = piece * 2 + mixed % 2
        mixed = mixed // 2
    return piece ^ ((col % per_home) % 2) * (row_count // 2)


def per_device(
    inverse,
    pattern,
    factor_first,
    factor_second,
    rows_first,
    rows_second,
    coupling,
    diag_first,
    diag_second,
):
    row_count = lax.axis_size("row")
    col_count = lax.axis_size("col")
    count = row_count * col_count
    row_index = lax.axis_index("row")
    col_index = lax.axis_index("col")
    me = row_index * col_count + col_index
    share_rows = factor_first.shape[0]
    quota_rows = inverse.shape[0] // col_count

    along, across = [], []
    for i in range(count):
        row, col = divmod(i, col_count)
        goal = col * row_count + piece_of(row, col, row_count, col_count)
        between = row * col_count + goal % col_count
        along.append((i, between))
        across.append((between, goal))
    start = piece_of(row_index, col_index, row_count, col_count) * quota_rows
    near = pick(start, quota_rows, factor_first, factor_second)
    near, (pattern,) = after(near, pattern)
    near = lax.ppermute(near, AXES, along)

    core = col_index & 1
    spare = bits_of(col_count) - 1
    forward = [2 << bit for bit in range(spare)]
    backward = list(reversed(forward))
    order = sorted(
        range(1 << spare), key=lambda e: -int(format(e, "b").zfill(spare)[::-1] or "0", 2)
    )

    places = []
    for e in order:
        offsets = [
            sum(bit for at, bit in enumerate(line) if e >> at & 1) for line in (forward, backward)
        ]
        for own in (0, 1):
            of_core = core if own else 1 - core
            places.append(
                col_index ^ core ^ of_core ^ jnp.where(of_core == 0, offsets[0], offsets[1])
            )
    plan = Plan(places, col_index * (share_rows // BLK), (rows_first, rows_second), pattern)

    last = len(order) - 1
    groups = [[(0, 0)]]
    for i in range(last - 1):
        groups.append([(i, 1), (i + 1, 0)])
    groups += [[(last - 1, 1)], [(last, 0)], [(last, 1)]]

    arrived = {e: [] for e in order}
    exchanged = {}
    split = None
    result = None
    for turn, group in enumerate(groups):
        if turn == len(groups) - 3:
            near, split = after(near, *split)
            near = lax.ppermute(near, AXES, across)
        at = [2 * i + own for i, own in group]
        if split is None:
            outs, split = product(plan, inverse, at, quota_rows, (factor_first, factor_second))
        else:
            outs = product(plan, inverse, at, quota_rows, None, split)
        for (i, own), out in zip(group, outs):
            e = order[i]
            if not own:
                exchanged[e] = flip(out, count, lambda i: 1)
                continue
            if i == last:
                result = [out, exchanged[e]] + arrived[e]
                continue
            out = functools.reduce(jnp.add, [out, exchanged[e]] + arrived[e])
            out, split = after(out, *split)
            bit = bits_of(e & -e)
            got = flip(out, count, lambda i: (backward if i & 1 else forward)[bit])
            arrived[e & (e - 1)].append(got)

    panel_one, panel_two, sums = finish(
        me * (quota_rows // BLK), near, rows_first, rows_second, coupling, result
    )

    digits = [(1, 2), (2, col_count // 2)]
    for stride, size in digits:
        spot = (me // stride) % size
        part = sums.shape[0] // size
        got = [lax.dynamic_slice_in_dim(sums, spot * part, part, 0)]
        for d in range(1, size):
            sent = lax.dynamic_slice_in_dim(sums, (spot ^ d) * part, part, 0)
            got.append(flip(sent, count, lambda i: d * stride))
        sums = tree_sum(got)
    for bit in range(bits_of(row_count)):
        sums = sums + flip(sums, count, lambda i: col_count << bit)
    for stride, size in reversed(digits):
        spot = (me // stride) % size
        got = [sums] + [flip(sums, count, lambda i: d * stride) for d in range(1, size)]
        sums = jnp.concatenate(
            [chosen(spot, [got[p ^ slot] for p in range(size)]) for slot in range(size)], axis=0
        )
    block_one, block_cross, block_two = close(sums, coupling, diag_first, diag_second)
    return (panel_one, panel_two, block_one, block_cross, block_two)


def solution(mesh):
    return jax.shard_map(
        per_device,
        mesh=mesh,
        in_specs=(
            P("row", "col"),
            P("row", "col"),
            P("col", None),
            P("col", None),
            P(),
            P(),
            P(),
            P(),
            P(),
        ),
        out_specs=(P(AXES, None), P(AXES, None), P(), P(), P()),
        check_vma=False,
    )
```
